512 devices in a mesh: frame: 32 (over y_lo, z), slab: 16 (over x, y_hi, core).
Axes of the slice: x: 4, y: 4 (y_hi: 2, y_lo: 2; y = y_hi * 2 + y_lo), z: 16, core: 2. Of those that a mesh axis runs over, the one named last changes fastest.
Arguments:
- pano: bfloat16 [512, 256, 320], P('frame', 'slab'), parts along dimension 0, may hold values from -6 to 6
- views: bfloat16 [1024, 16, 16, 320], P(('frame', 'slab')), parts along dimension 0, may hold values from -6 to 6
- view_count: int32 [512], P('frame'), parts along dimension 0, may hold values from 0 to 2, as said below
- links: int32 [1024, 2], P('frame'), parts along dimension 0, may hold values from 0 to 2
- pano_conv1: bfloat16 [9, 320, 320], P(None, 'slab'), may hold values from -0.109375 to 0.109375
- pano_conv2: bfloat16 [9, 320, 320], P(None, 'slab'), may hold values from -0.109375 to 0.109375
- view_conv1: bfloat16 [9, 320, 320], P(None, 'slab'), may hold values from -0.109375 to 0.109375
- view_conv2: bfloat16 [9, 320, 320], P(None, 'slab'), may hold values from -0.109375 to 0.109375
- p2v_query: bfloat16 [320, 320], replicated, may hold values from -0.6 to 0.6
- p2v_key: bfloat16 [320, 320], replicated, may hold values from -0.6 to 0.6
- p2v_value: bfloat16 [320, 320], replicated, may hold values from -0.3125 to 0.3125
- p2v_out: bfloat16 [320, 320], replicated, may hold values from -0.3125 to 0.3125
- v2p_query: bfloat16 [320, 320], replicated, may hold values from -0.6 to 0.6
- v2p_key: bfloat16 [320, 320], replicated, may hold values from -0.6 to 0.6
- v2p_value: bfloat16 [320, 320], replicated, may hold values from -0.3125 to 0.3125
- v2p_out: bfloat16 [320, 320], replicated, may hold values from -0.3125 to 0.3125
Outputs:
- pano_out: bfloat16 [512, 256, 320], P('frame', 'slab'), parts along dimension 0
- view_out: bfloat16 [1024, 16, 16, 320], P(('frame', 'slab')), parts along dimension 0
The draws below stay inside these ranges and needn't reach their ends.
There are 32 independent parts, one for each index of `frame`. The reference program is written for one: setup_inputs(seed, part) draws one part's arguments, and reference() takes and returns one part's arrays. A program takes and returns all parts, laid end to end along the dimension named above; an argument that names none is the same for every part. Nothing has to cross between parts.
Inputs may be any that keep to these rules, and one draw needn't show every extreme that they name: `view_count`: in every frame some slab has no occupied slot and some has 2.
All inputs are finite; a program needn't handle non-finite values.
Results may differ from the reference program's by a relative error of at most 0.0085.
Values may be sent and summed in bfloat16 or wider, within the bound.
A program may use at most 64 MiB of HBM per device.

```python
import jax
import jax.numpy as jnp
from jax import lax

C = 320
HEADS = 5
PR = 16
BLOCK = 16
SLOTS = 2
LINKS = 2
BANDS = 1
LON = 256
VIEW_SLOTS = 32
N_SLAB = 16


def drawn_weight(key, which):
    base = jax.random.normal(jax.random.fold_in(key, 101 + which), (C, C), jnp.float32) * C ** (-0.5)
    base = jnp.clip(base, -0.4, 0.4)
    return base.astype(jnp.bfloat16)


def drawn_tokens(key, shape):
    drawn = jnp.clip(jax.random.normal(jax.random.fold_in(key, 11), shape, jnp.float32), -6.0, 6.0)
    return drawn.astype(jnp.bfloat16)


def draw_pano(key, part):
    return drawn_tokens(jax.random.fold_in(key, 21), (PR, LON, C))


def draw_views(key, part):
    return drawn_tokens(jax.random.fold_in(key, 22), (VIEW_SLOTS, BLOCK, BLOCK, C))


def draw_p2v_query(key, part):
    return drawn_weight(key, 1)


def draw_p2v_key(key, part):
    return drawn_weight(key, 2)


def draw_v2p_query(key, part):
    return drawn_weight(key, 3)


def draw_v2p_key(key, part):
    return drawn_weight(key, 4)


def draw_view_count(key, part):
    counts = jax.random.randint(jax.random.fold_in(key, 7), (N_SLAB,), 0, SLOTS + 1)
    order = jax.random.permutation(jax.random.fold_in(key, 8), N_SLAB)
    counts = counts.at[order[0]].set(0).at[order[1]].set(SLOTS)
    return counts.astype(jnp.int32)


def with_ends(values, stream_key, least, largest):
    longest = values.shape.index(max(values.shape))
    spots = []
    for shift in (0, 1):
        where = [jax.random.randint(jax.random.fold_in(stream_key, axis), (), 0, length) for axis, length in enumerate(values.shape)]
        where[longest] = (where[longest] + shift) % values.shape[longest]
        spots.append(tuple(where))
    return values.at[spots[0]].set(least).at[spots[1]].set(largest)


def block_scale(key, dims, split, least, top_value):
    def one(axis_at, parts):
        steps = jax.random.uniform(jax.random.fold_in(jax.random.fold_in(key, 6), axis_at), (parts,), jnp.float32, least / len(split), top_value / len(split))
        return jnp.repeat(jnp.exp(steps), dims[axis_at] // parts).reshape((-1,) + (1,) * (len(dims) - axis_at - 1))

    loudness = one(*split[0])
    for cut in split[1:]:
        loudness = loudness * one(*cut)
    return loudness


def noise(stream_key, dims, width, bound, split=(), held_as=jnp.bfloat16):
    drawn = width * jax.random.normal(stream_key, dims, jnp.float32)
    if split:
        drawn = drawn * block_scale(stream_key, dims, split, -0.22, 0.18)
    return jnp.clip(drawn, -bound, bound).astype(held_as)


def setup_inputs(seed: int = 0, part: int = 0) -> dict:
    arg_keys = jax.random.split(jax.random.key(seed), 17)
    part_splits = jax.random.split(jax.random.fold_in(arg_keys[16], part), 17)
    return {
        "pano": draw_pano(jax.random.fold_in(jax.random.fold_in(arg_keys[16], part), 71), part),
        "views": draw_views(jax.random.fold_in(jax.random.fold_in(arg_keys[16], part), 71), part),
        "view_count": draw_view_count(jax.random.fold_in(jax.random.fold_in(arg_keys[16], part), 71), part),
        "links": with_ends(jax.random.randint(part_splits[3], (VIEW_SLOTS, LINKS), 0, 3 * BANDS), jax.random.fold_in(part_splits[3], 1), 0, (3 * BANDS) - 1).astype(jnp.int32),
        "pano_conv1": noise(arg_keys[4], (9, C, C), (9 * C) ** -0.5, 0.109375, ((1, 16),)),
        "pano_conv2": noise(arg_keys[5], (9, C, C), (9 * C) ** -0.5, 0.109375, ((1, 16),)),
        "view_conv1": noise(arg_keys[6], (9, C, C), (9 * C) ** -0.5, 0.109375, ((1, 16),)),
        "view_conv2": noise(arg_keys[7], (9, C, C), (9 * C) ** -0.5, 0.109375, ((1, 16),)),
        "p2v_query": draw_p2v_query(jax.random.fold_in(arg_keys[16], 71), part),
        "p2v_key": draw_p2v_key(jax.random.fold_in(arg_keys[16], 71), part),
        "p2v_value": noise(arg_keys[10], (C, C), C ** -0.5, 0.3125),
        "p2v_out": noise(arg_keys[11], (C, C), C ** -0.5, 0.3125),
        "v2p_query": draw_v2p_query(jax.random.fold_in(arg_keys[16], 71), part),
        "v2p_key": draw_v2p_key(jax.random.fold_in(arg_keys[16], 71), part),
        "v2p_value": noise(arg_keys[14], (C, C), C ** -0.5, 0.3125),
        "v2p_out": noise(arg_keys[15], (C, C), C ** -0.5, 0.3125),
    }


def tap_stack(padded, lat_rows, lon_cols):
    shifted = [padded[..., row_step:row_step + lat_rows, col_step:col_step + lon_cols, :] for row_step in range(3) for col_step in range(3)]
    return jnp.stack(shifted, axis=-2)


def conv_apply(columns, weight):
    return jnp.einsum("...kc,kcd->...d", columns.astype(jnp.float32), weight.astype(jnp.float32))


def cycle_conv(feature, weight):
    padded = jnp.pad(feature, ((1, 1), (0, 0), (0, 0)))
    padded = jnp.concatenate([padded[:, -1:], padded, padded[:, :1]], axis=1)
    return conv_apply(tap_stack(padded, feature.shape[0], feature.shape[1]), weight)


def flat_conv(feature, weight):
    padded = jnp.pad(feature, ((0, 0), (1, 1), (1, 1), (0, 0)))
    return conv_apply(tap_stack(padded, feature.shape[1], feature.shape[2]), weight)


def project(feature, weight):
    return jnp.einsum("...c,cd->...d", feature.astype(jnp.float32), weight.astype(jnp.float32)).astype(jnp.bfloat16)


def reference(pano, views, view_count, links, pano_conv1, pano_conv2, view_conv1, view_conv2,
              p2v_query, p2v_key, p2v_value, p2v_out, v2p_query, v2p_key, v2p_value, v2p_out):
    head_width = C // HEADS
    scaling = head_width ** -0.5
    band_count = PR // BLOCK
    view_tokens = BLOCK * BLOCK

    def to_blocks(array):
        shaped = array.reshape(band_count, BLOCK, N_SLAB, BLOCK, array.shape[-1])
        return shaped.transpose(2, 0, 1, 3, 4).reshape(N_SLAB, band_count, view_tokens, array.shape[-1])

    def from_blocks(array):
        shaped = array.reshape(N_SLAB, band_count, BLOCK, BLOCK, array.shape[-1])
        return shaped.transpose(1, 2, 0, 3, 4).reshape(PR, LON, array.shape[-1])

    pano_hidden = jax.nn.silu(cycle_conv(pano, pano_conv1)).astype(jnp.bfloat16)
    pano_mid = pano.astype(jnp.float32) + cycle_conv(pano_hidden, pano_conv2)
    view_hidden = jax.nn.silu(flat_conv(views, view_conv1)).astype(jnp.bfloat16)
    view_mid = views.astype(jnp.float32) + flat_conv(view_hidden, view_conv2)
    pano_feat = pano_mid.astype(jnp.bfloat16)
    view_feat = view_mid.astype(jnp.bfloat16).reshape(N_SLAB, SLOTS, view_tokens, C)

    pano_query = to_blocks(project(pano_feat, p2v_query)).reshape(N_SLAB, band_count, view_tokens, HEADS, head_width)
    pano_pairs = to_blocks(project(pano_feat, jnp.concatenate([v2p_key, v2p_value], axis=1)))
    view_query = project(view_feat, v2p_query).reshape(N_SLAB, SLOTS, view_tokens, HEADS, head_width)
    view_pairs = project(view_feat, jnp.concatenate([p2v_key, p2v_value], axis=1))

    slab_links = links.reshape(N_SLAB, SLOTS, LINKS)
    source = (jnp.arange(N_SLAB, dtype=jnp.int32)[:, None, None] + slab_links // band_count - 1) % N_SLAB
    band_index = slab_links % band_count
    chosen = pano_pairs[source, band_index].reshape(N_SLAB, SLOTS, LINKS * view_tokens, 2 * C)
    key_rows = chosen[..., :C].reshape(N_SLAB, SLOTS, LINKS * view_tokens, HEADS, head_width).astype(jnp.float32)
    value_rows = chosen[..., C:].reshape(N_SLAB, SLOTS, LINKS * view_tokens, HEADS, head_width).astype(jnp.float32)
    scores = jnp.einsum("nsqhd,nskhd->nshqk", view_query.astype(jnp.float32), key_rows) * scaling
    highest = jnp.max(scores, axis=-1, keepdims=True)
    weights = jnp.exp(scores - highest)
    shares = (weights / jnp.sum(weights, axis=-1, keepdims=True)).astype(jnp.bfloat16)
    attended = jnp.einsum("nshqk,nskhd->nsqhd", shares.astype(jnp.float32), value_rows).astype(jnp.bfloat16)
    attended = attended.reshape(N_SLAB, SLOTS, view_tokens, C)
    view_delta = jnp.einsum("nstc,cd->nstd", attended.astype(jnp.float32), v2p_out.astype(jnp.float32))
    occupied = jnp.arange(SLOTS, dtype=jnp.int32)[None, :] < view_count[:, None]
    view_total = view_mid.reshape(N_SLAB, SLOTS, view_tokens, C) + view_delta
    view_out = jnp.where(occupied[:, :, None, None], view_total, 0.0).astype(jnp.bfloat16).reshape(views.shape)

    nearby = jnp.concatenate([jnp.roll(view_pairs, 1, axis=0), view_pairs, jnp.roll(view_pairs, -1, axis=0)], axis=1)
    nearby = nearby.reshape(N_SLAB, 3 * SLOTS * view_tokens, 2 * C)
    near_links = jnp.stack([jnp.roll(slab_links, 1, axis=0), slab_links, jnp.roll(slab_links, -1, axis=0)], axis=1)
    near_counts = jnp.stack([jnp.roll(view_count, 1), view_count, jnp.roll(view_count, -1)], axis=1)
    wanted = (2 - jnp.arange(3, dtype=jnp.int32))[:, None, None, None] * band_count + jnp.arange(band_count, dtype=jnp.int32)[None, None, None, :]
    linked = jnp.any(near_links[..., None] == wanted[None], axis=3)
    present = jnp.arange(SLOTS, dtype=jnp.int32)[None, None, :] < near_counts[:, :, None]
    allowed = (linked & present[..., None]).transpose(0, 3, 1, 2).reshape(N_SLAB, band_count, 3 * SLOTS)
    allowed = jnp.repeat(allowed, view_tokens, axis=2)

    def one_slab(operands):
        query, pairs, permitted = operands
        near_keys = pairs[:, :C].reshape(-1, HEADS, head_width).astype(jnp.float32)
        near_values = pairs[:, C:].reshape(-1, HEADS, head_width).astype(jnp.float32)
        slab_scores = jnp.einsum("rqhd,khd->rhqk", query.astype(jnp.float32), near_keys) * scaling
        mask_rows = permitted[:, None, None, :]
        slab_top = jnp.maximum(jnp.max(jnp.where(mask_rows, slab_scores, -jnp.inf), axis=-1, keepdims=True), 0.0)
        slab_weights = jnp.where(mask_rows, jnp.exp(slab_scores - slab_top), 0.0)
        slab_total = jnp.sum(slab_weights, axis=-1, keepdims=True) + jnp.exp(-slab_top)
        slab_shares = (slab_weights / slab_total).astype(jnp.bfloat16)
        result = jnp.einsum("rhqk,khd->rqhd", slab_shares.astype(jnp.float32), near_values)
        return result.astype(jnp.bfloat16).reshape(band_count, view_tokens, C)

    pano_attended = from_blocks(lax.map(one_slab, (pano_query, nearby, allowed)))
    pano_delta = jnp.einsum("rwc,cd->rwd", pano_attended.astype(jnp.float32), p2v_out.astype(jnp.float32))
    pano_out = (pano_mid + pano_delta).astype(jnp.bfloat16)
    return pano_out, view_out
```

```python
import jax
import jax.numpy as jnp
import numpy as np
from jax import lax
from jax.experimental import pallas as pl
from jax.experimental.pallas import tpu as pltpu
from jax.sharding import PartitionSpec as P

MESH = pl.DeviceIdType.MESH
F32, BF = jnp.float32, jnp.bfloat16
HEADS, C, CP, TOK = 5, 320, 384, 256
SHARD = 192
NEG = -1e30

XP0, XP1, XM0, XM1, XP2, XM2 = range(6)
OPP, FAN, SIB, PER_PAIR = 6, 10, 22, 30
HALO, VIEWS, PANO, N_SEM = 60, 62, 64, 66


def rest_order(pair):
    order = [(0, 0), (1, 0), (0, 1), (1, 1), (0, 2), (1, 2), (2, 0), (2, 1), (2, 2)]
    return [3 * b + a if pair == 0 else 3 * a + b for a, b in order]


def tap_shift(pair, tap):
    return (tap % 3, tap // 3) if pair == 0 else (tap // 3, tap % 3)


def turn_matrix():
    m = np.zeros((TOK, TOK), np.float32)
    for r in range(TOK):
        m[r, (r % 16) * 16 + r // 16] = 1
    return m


def join_matrix():
    m = np.zeros((240, 256), np.float32)
    for r in range(240):
        tap, u = r // 80, r % 80
        m[r, (u // 20) * 64 + tap * 20 + u % 20] = 1
    return m


def kernel(
    wp, pano, views, count, links, turn, join,
    p2v_q, p2v_k, p2v_v, p2v_o, v2p_q, v2p_k, v2p_v, v2p_o,
    pano_out, view_out,
    sh, wm, wr, main, rc, r2, xpad, xext, vmid, pmid, vf, pf, wks, wvs, kv, vv, kp, vp, qs, att, ss, rs,
):
    s, f = lax.axis_index("slab"), lax.axis_index("frame")
    x, h, c = lax.div(s, 4), lax.rem(lax.div(s, 2), 2), lax.rem(s, 2)
    l, z = lax.div(f, 16), lax.rem(f, 16)
    xm, xp, xx = lax.rem(x + 3, 4), lax.rem(x + 1, 4), lax.rem(x + 2, 4)
    xs = (x, xm, xp, xx)

    def dev(x_, h_, c_, l_, z_):
        return (l_ * 16 + z_, x_ * 4 + h_ * 2 + c_)

    to_xp, to_xm = dev(xp, h, c, l, z), dev(xm, h, c, l, z)
    opposite, same = dev(x, 1 - h, c, 1 - l, z), dev(x, h, c, 1 - l, z)
    to_zp, to_zm = dev(x, h, c, l, lax.rem(z + 1, 16)), dev(x, h, c, l, lax.rem(z + 15, 16))
    sibling = dev(x, h, 1 - c, l, z)
    beyond = (f, lax.rem(s + 15 + 2 * c, 16))
    fans = (same, to_zp, to_zm)

    barrier = pltpu.get_barrier_semaphore()
    for d in (to_xp, to_xm, opposite, same, to_zp, to_zm, sibling, beyond):
        pl.semaphore_signal(barrier, inc=1, device_id=d, device_id_type=MESH)

    sent = []

    def copy(i, to, src, dst):
        return pltpu.make_async_remote_copy(
            src_ref=src, dst_ref=dst, send_sem=ss.at[i], recv_sem=rs.at[i], device_id=to, device_id_type=MESH
        )

    def send(i, to, src, dst=None):
        cp = copy(i, to, src, src if dst is None else dst)
        cp.start()
        sent.append(cp)

    def recv(i, dst):
        copy(i, sibling, dst, dst).wait_recv()

    def rows(q, x_, h_, c_, start, n):
        return sh.at[q, x_ * 4 + h_ * 2 + c_, pl.ds(start, n)]

    colour = lax.rem(z + 2 * l, 4)

    def quarter(q, x_, h_, k):
        return rows(q, x_, h_, c, pl.multiple_of(lax.rem(k, 4) * 48, 16), 48)

    def whole(q, x_, h_, c_):
        return sh.at[q, x_ * 4 + h_ * 2 + c_]

    def start_own(q):
        b = q * PER_PAIR
        send(b + XP0, to_xp, rows(q, x, h, c, 0, 96))
        send(b + XM0, to_xm, rows(q, x, h, c, 96, 96))
        send(b + XP1, to_xp, rows(q, x, h, c, 96, 96))
        send(b + XM1, to_xm, rows(q, x, h, c, 0, 96))
        send(b + OPP, opposite, quarter(q, x, h, colour + 2))
        send(b + SIB, sibling, whole(q, x, h, c))

    def second_hop(q):
        b = q * PER_PAIR
        recv(b + XP0, rows(q, xm, h, c, 0, 96))
        send(b + XP2, to_xp, rows(q, xm, h, c, 0, 96))
        recv(b + XM0, rows(q, xp, h, c, 96, 96))
        send(b + XM2, to_xm, rows(q, xp, h, c, 96, 96))

    def pass_on(q, j):
        b = q * PER_PAIR
        send(b + OPP + j, opposite, quarter(q, xs[j], h, colour + 2))
        send(b + SIB + j, sibling, whole(q, xs[j], h, c))

    def first_done(q):
        b = q * PER_PAIR
        recv(b + XP1, rows(q, xm, h, c, 96, 96))
        pass_on(q, 1)
        recv(b + XM1, rows(q, xp, h, c, 0, 96))
        pass_on(q, 2)

    def second_done(q):
        b = q * PER_PAIR
        recv(b + XP2, rows(q, xx, h, c, 0, 96))
        recv(b + XM2, rows(q, xx, h, c, 96, 96))
        pass_on(q, 3)

    def fan_out(q, j):
        b = q * PER_PAIR
        recv(b + OPP + j, quarter(q, xs[j], 1 - h, colour))
        for d in range(3):
            send(b + FAN + 4 * d + j, fans[d], quarter(q, xs[j], 1 - h, colour))

    def fanned(q, j):
        b = q * PER_PAIR
        for d, k in enumerate((2, 3, 1)):
            recv(b + FAN + 4 * d + j, quarter(q, xs[j], 1 - h, colour + k))
        send(b + SIB + 4 + j, sibling, whole(q, xs[j], 1 - h, c))

    def all_here(q):
        b = q * PER_PAIR
        for j in range(4):
            recv(b + SIB + j, whole(q, xs[j], h, 1 - c))
            recv(b + SIB + 4 + j, whole(q, xs[j], 1 - h, 1 - c))

    def dot(a, b):
        return jnp.dot(a, b, preferred_element_type=F32)

    def join_up(q):
        place = {tap: i for i, tap in enumerate(rest_order(q))}
        for x_ in range(4):
            for g in range(3):
                parts = jnp.concatenate([sh[q, 4 * x_ + i, 64 * g : 64 * g + 64, :] for i in range(4)], axis=0)
                joined = dot(join[...], parts).astype(BF)
                for k in range(3):
                    tap, block = 3 * g + k, joined[80 * k : 80 * k + 80]
                    if x_ < 3:
                        wm[q, 256 * tap + 80 * x_ : 256 * tap + 80 * x_ + 80, :] = block
                    else:
                        wm[q, 256 * tap + 240 : 256 * tap + 256, :] = block[:16]
                        wr[q, 64 * place[tap] : 64 * place[tap] + 64, :] = block[16:]

    def prepare(a, n):
        row = lax.broadcasted_iota(jnp.int32, (n, CP), 0) & 15
        moved = (
            jnp.where(row == 0, 0.0, pltpu.roll(a, 1, 0)),
            a,
            jnp.where(row == 15, 0.0, pltpu.roll(a, n - 1, 0)),
        )
        for i in range(3):
            main[i, :n, :] = moved[i][:, :256].astype(BF)
        t0, t1, t2 = (m[:, 256:] for m in moved)
        rc[:n, :] = (t0 + pltpu.roll(t1, 64, 1)).astype(BF)
        later = jnp.concatenate([t2[16:], t2[:16]], axis=0)
        r2[:n, :] = (t2 + pltpu.roll(later, 64, 1)).astype(BF)

    def conv(q, second, m):
        lo = 256 if second else 0
        left = []
        for tap in range(9):
            a, b = tap_shift(q, tap)
            left.append(main[a, 16 * b : 16 * b + m, :])
        acc = dot(jnp.concatenate(left, axis=1), wm[q, :, lo : lo + CP])
        rest = [rc[16 * b : 16 * b + m, :] for b in range(3)] + [r2[:m, :], r2[32 : 32 + m, :64]]
        acc += dot(jnp.concatenate(rest, axis=1), wr[q, :, lo : lo + CP])
        if second:
            acc = pltpu.roll(acc, C, 1)
        return jnp.where(lax.broadcasted_iota(jnp.int32, (m, CP), 1) < C, acc, 0.0)

    def silu(v):
        return v / (1.0 + jnp.exp(-v))

    def view_first(v):
        xpad[16:272, :C] = views[TOK * v : TOK * v + TOK, :].astype(F32)
        xpad[16:272, C:] = jnp.zeros((TOK, CP - C), F32)
        prepare(xpad[:288, :], 288)
        xpad[16:272, :] = silu(conv(0, False, TOK))

    def view_second(v):
        prepare(xpad[:288, :], 288)
        acc = conv(0, True, TOK)
        vmid[v, :, :] = acc
        vmid[v, :, :C] = acc[:, :C] + views[TOK * v : TOK * v + TOK, :].astype(F32)

    def put_values(to, g, val):
        val = val.astype(BF)
        to[g, :, 0:128] = val[:, :128]
        to[g, :, 256:384] = val[:, 128:256]
        to[g, :, 512:576] = val[:, 256:320]

    def view_pairs(o):
        first, second = vf[o, :, :C], vf[o, :, 256:]
        kv[2 * o, :, :C] = dot(first, p2v_k[...]).astype(BF)
        put_values(vv, 2 * o, dot(first, p2v_v[...]))
        kv[2 * o + 1, :, :C] = dot(second, wks[...]).astype(BF)
        put_values(vv, 2 * o + 1, dot(second, wvs[...]))

    def pano_pairs(o):
        feat = pf[o, :, :C]
        kp[o, :, :C] = dot(feat, v2p_k[...]).astype(BF)
        put_values(vp, o, dot(feat, v2p_v[...]))

    def attend(keys, values, bias, sink):
        lane = lax.broadcasted_iota(jnp.int32, (TOK, 128), 1)
        for j in range(3):
            query, ks = qs[:, 128 * j : 128 * j + 128], keys(j)
            vs = jnp.concatenate(values(j), axis=0)
            halves = []
            for e in range(2 if j < 2 else 1):
                mine = (lane >= 64 * e) & (lane < 64 * e + 64)
                picked = jnp.where(mine, query, jnp.zeros_like(query))
                scores = [
                    lax.dot_general(picked, k, (((1,), (1,)), ((), ())), preferred_element_type=F32) for k in ks
                ]
                top = None
                for sc, b in zip(scores, bias, strict=True):
                    t = jnp.max(sc, axis=1, keepdims=True)
                    t = t if b is None else t + b
                    top = t if top is None else jnp.maximum(top, t)
                if sink:
                    top = jnp.maximum(top, 0.0)
                shares = [
                    jnp.exp(sc - (top if b is None else top - b)).astype(BF) for sc, b in zip(scores, bias, strict=True)
                ]
                both = dot(jnp.concatenate(shares, axis=1), vs)
                total = both[:, 128:]
                if sink:
                    total = total + jnp.exp(-top)
                halves.append(both[:, :128] / total)
            out = halves[0] if j == 2 else jnp.where(lane < 64, halves[0], halves[1])
            att[:, 128 * j : 128 * j + 128] = out.astype(BF)

    sh[0, s] = wp[0]
    sh[1, s] = wp[1]
    xext[32:288, 256:] = jnp.zeros((TOK, 128), BF)
    xext[32:288, :C] = dot(turn[...], pano[...]).astype(BF)
    pl.semaphore_wait(barrier, 8)
    start_own(0)
    send(HALO, sibling, xext.at[pl.ds(pl.multiple_of(32 + 224 * (1 - c), 16), 32)],
         xext.at[pl.ds(pl.multiple_of(288 * c, 16), 32)])
    send(HALO + 1, beyond, xext.at[pl.ds(pl.multiple_of(32 + 224 * c, 16), 32)],
         xext.at[pl.ds(pl.multiple_of(288 * (1 - c), 16), 32)])

    xpad[0:16, :] = jnp.zeros((16, CP), F32)
    xpad[272:288, :] = jnp.zeros((16, CP), F32)
    for buf, n in ((kv, 6), (kp, 3)):
        for g in range(n):
            buf[g, :, 256:] = jnp.zeros((TOK, 128), BF)
    for buf, n in ((vv, 6), (vp, 3)):
        for g in range(n):
            for j in range(3):
                buf[g, :, 256 * j + 128 : 256 * j + 256] = jnp.ones((TOK, 128), BF)
            buf[g, :, 512:640] = jnp.zeros((TOK, 128), BF)
    qs[:, 256:] = jnp.zeros((TOK, 128), BF)
    for to, w in ((wks, p2v_k), (wvs, p2v_v)):
        to[0:64, :] = jnp.zeros((64, C), BF)
        to[64:384, :] = w[...]

    second_hop(0)
    start_own(1)
    first_done(0)
    for j in range(3):
        fan_out(0, j)
    second_done(0)
    fan_out(0, 3)
    second_hop(1)
    for j in range(4):
        fanned(0, j)
    first_done(1)
    all_here(0)

    join_up(0)
    view_first(0)
    fan_out(1, 0)
    fan_out(1, 1)
    fan_out(1, 2)
    view_second(0)
    second_done(1)
    view_first(1)
    fan_out(1, 3)
    for j in range(3):
        fanned(1, j)
    view_second(1)
    fanned(1, 3)
    f0, f1 = vmid[0], pltpu.roll(vmid[1], 64, 1)
    vf[1, :, :256] = f0[:, :256].astype(BF)
    vf[1, :, 256:384] = (f0[:, 256:] + f1[:, :128]).astype(BF)
    vf[1, :, 384:] = f1[:, 128:].astype(BF)
    send(VIEWS, sibling, vf.at[1], vf.at[2 * c])
    send(VIEWS + 1, beyond, vf.at[1], vf.at[2 * (1 - c)])
    view_pairs(1)

    recv(HALO, xext.at[pl.ds(pl.multiple_of(288 * (1 - c), 16), 32)])
    recv(HALO + 1, xext.at[pl.ds(pl.multiple_of(288 * c, 16), 32)])
    prepare(xext[...].astype(F32), 320)
    all_here(1)
    join_up(1)
    hidden = silu(conv(1, False, 288))
    prepare(hidden, 288)
    mid = conv(1, True, TOK) + xext[32:288, :].astype(F32)
    pmid[...] = mid
    pf[1] = mid.astype(BF)
    send(PANO, sibling, pf.at[1], pf.at[2 * c])
    send(PANO + 1, beyond, pf.at[1], pf.at[2 * (1 - c)])
    pano_pairs(1)

    recv(VIEWS, vf.at[2 * (1 - c)])
    recv(VIEWS + 1, vf.at[2 * c])
    view_pairs(0)
    view_pairs(2)
    qs[:, :C] = (dot(pf[1, :, :C], p2v_q[...]).astype(BF).astype(F32) * 0.125).astype(BF)
    bias = []
    for o in range(3):
        so = lax.rem(s + 15 + o, 16)
        for v in range(2):
            named = (links[2 * so + v, 0] == 2 - o) | (links[2 * so + v, 1] == 2 - o)
            bias.append(jnp.where(named & (count[so] > v), 0.0, NEG))
    attend(
        lambda j: [kv[g, :, 128 * j : 128 * j + 128] for g in range(6)],
        lambda j: [vv[g, :, 256 * j : 256 * j + 256] for g in range(6)],
        bias,
        True,
    )
    total = pmid[:, :C] + dot(att[:, :C], p2v_o[...])
    pano_out[...] = dot(turn[...], total.astype(BF)).astype(BF)

    recv(PANO, pf.at[2 * (1 - c)])
    recv(PANO + 1, pf.at[2 * c])
    pano_pairs(0)
    pano_pairs(2)
    for v in range(2):
        feat = vmid[v, :, :C].astype(BF)
        qs[:, :C] = (dot(feat, v2p_q[...]).astype(BF).astype(F32) * 0.125).astype(BF)
        a, b = links[2 * s + v, 0], links[2 * s + v, 1]
        attend(
            lambda j: [kp[i, :, 128 * j : 128 * j + 128] for i in (a, b)],
            lambda j: [vp[i, :, 256 * j : 256 * j + 256] for i in (a, b)],
            [None, None],
            False,
        )
        total = vmid[v, :, :C] + dot(att[:, :C], v2p_o[...])
        total = total * jnp.where(count[s] > v, 1.0, 0.0)
        view_out[TOK * v : TOK * v + TOK, :] = total.astype(BF)

    for cp in sent:
        cp.wait_send()


def packed(first, second):
    both = jnp.concatenate([first, second], axis=2).reshape(3, 60, 2 * C)
    return jnp.pad(both, ((0, 0), (0, 4), (0, 0))).reshape(SHARD, 2 * C)


def body(pano, views, count, links, pc1, pc2, vc1, vc2, *projections):
    wp = jnp.stack([packed(vc1, vc2), packed(pc1, pc2)])
    vmem, smem = pl.BlockSpec(memory_space=pltpu.VMEM), pl.BlockSpec(memory_space=pltpu.SMEM)
    pano_out, view_out = pl.pallas_call(
        kernel,
        out_shape=(jax.ShapeDtypeStruct((TOK, C), BF), jax.ShapeDtypeStruct((2 * TOK, C), BF)),
        in_specs=[vmem] * 3 + [smem] * 2 + [vmem] * 10,
        out_specs=(vmem, vmem),
        scratch_shapes=[
            pltpu.VMEM((2, 16, SHARD, 2 * C), BF),
            pltpu.VMEM((2, 9 * 256, 2 * C), BF),
            pltpu.VMEM((2, 9 * 64, 2 * C), BF),
            pltpu.VMEM((3, 320, 256), BF),
            pltpu.VMEM((320, 128), BF),
            pltpu.VMEM((320, 128), BF),
            pltpu.VMEM((288, CP), F32),
            pltpu.VMEM((320, CP), BF),
            pltpu.VMEM((2, TOK, CP), F32),
            pltpu.VMEM((TOK, CP), F32),
            pltpu.VMEM((3, TOK, 2 * C), BF),
            pltpu.VMEM((3, TOK, CP), BF),
            pltpu.VMEM((CP, C), BF),
            pltpu.VMEM((CP, C), BF),
            pltpu.VMEM((6, TOK, CP), BF),
            pltpu.VMEM((6, TOK, 768), BF),
            pltpu.VMEM((3, TOK, CP), BF),
            pltpu.VMEM((3, TOK, 768), BF),
            pltpu.VMEM((TOK, CP), BF),
            pltpu.VMEM((TOK, CP), BF),
            pltpu.SemaphoreType.DMA((N_SEM,)),
            pltpu.SemaphoreType.DMA((N_SEM,)),
        ],
        compiler_params=pltpu.CompilerParams(
            collective_id=0, has_side_effects=True, vmem_limit_bytes=56 * 1024 * 1024
        ),
    )(
        wp, pano.reshape(TOK, C), views.reshape(2 * TOK, C), count, links,
        jnp.asarray(turn_matrix(), BF), jnp.asarray(join_matrix(), BF), *projections,
    )
    return pano_out.reshape(pano.shape), view_out.reshape(views.shape)


def solution(mesh):
    in_specs = (
        P("frame", "slab", None),
        P(("frame", "slab"), None, None, None),
        P("frame"),
        P("frame", None),
        *[P(None, "slab", None)] * 4,
        *[P()] * 8,
    )
    out_specs = (P("frame", "slab", None), P(("frame", "slab"), None, None, None))
    return jax.shard_map(body, mesh=mesh, in_specs=in_specs, out_specs=out_specs, check_vma=False)
```

```python
import jax
import jax.numpy as jnp
import numpy as np
from jax import lax
from jax.experimental import pallas as pl
from jax.experimental.pallas import tpu as pltpu
from jax.sharding import PartitionSpec as P

MESH = pl.DeviceIdType.MESH
F32, BF = jnp.float32, jnp.bfloat16
HEADS, C, CP, TOK = 5, 320, 384, 256
SHARD = 192
NEG = -1e30

XP0, XP1, XM0, XM1, XP2, XM2 = range(6)
OPP, FAN, SIB, PER_PAIR = 6, 10, 22, 30
HALO, VIEWS, PANO, N_SEM = 60, 62, 64, 66


def rest_order(pair):
    order = [(0, 0), (1, 0), (0, 1), (1, 1), (0, 2), (1, 2), (2, 0), (2, 1), (2, 2)]
    return [3 * b + a if pair == 0 else 3 * a + b for a, b in order]


def tap_shift(pair, tap):
    return (tap % 3, tap // 3) if pair == 0 else (tap // 3, tap % 3)


def turn_matrix():
    m = np.zeros((TOK, TOK), np.float32)
    for r in range(TOK):
        m[r, (r % 16) * 16 + r // 16] = 1
    return m


def join_matrix():
    m = np.zeros((240, 256), np.float32)
    for r in range(240):
        tap, u = r // 80, r % 80
        m[r, (u // 20) * 64 + tap * 20 + u % 20] = 1
    return m


def kernel(
    pc1, pc2, vc1, vc2, pano, views, count, links, turn, join, spread,
    p2v_q, p2v_k, p2v_v, p2v_o, v2p_q, v2p_k, v2p_v, v2p_o,
    pano_out, view_out,
    sh, wm, wr, main, rc, r2, xpad, xext, vmid, pmid, vf, pf, wks, wvs, kv, vv, kp, vp, qs, att, ss, rs,
):
    s, f = lax.axis_index("slab"), lax.axis_index("frame")
    x, h, c = lax.div(s, 4), lax.rem(lax.div(s, 2), 2), lax.rem(s, 2)
    l, z = lax.div(f, 16), lax.rem(f, 16)
    xm, xp, xx = lax.rem(x + 3, 4), lax.rem(x + 1, 4), lax.rem(x + 2, 4)
    xs = (x, xm, xp, xx)

    def dev(x_, h_, c_, l_, z_):
        return (l_ * 16 + z_, x_ * 4 + h_ * 2 + c_)

    to_xp, to_xm = dev(xp, h, c, l, z), dev(xm, h, c, l, z)
    opposite, same = dev(x, 1 - h, c, 1 - l, z), dev(x, h, c, 1 - l, z)
    to_zp, to_zm = dev(x, h, c, l, lax.rem(z + 1, 16)), dev(x, h, c, l, lax.rem(z + 15, 16))
    sibling = dev(x, h, 1 - c, l, z)
    beyond = (f, lax.rem(s + 15 + 2 * c, 16))
    fans = (same, to_zp, to_zm)

    barrier = pltpu.get_barrier_semaphore()
    for d in (to_xp, to_xm, opposite, same, to_zp, to_zm, sibling, beyond):
        pl.semaphore_signal(barrier, inc=1, device_id=d, device_id_type=MESH)

    sent = []

    def copy(i, to, src, dst):
        return pltpu.make_async_remote_copy(
            src_ref=src, dst_ref=dst, send_sem=ss.at[i], recv_sem=rs.at[i], device_id=to, device_id_type=MESH
        )

    def send(i, to, src, dst=None):
        cp = copy(i, to, src, src if dst is None else dst)
        cp.start()
        sent.append(cp)

    def recv(i, dst):
        copy(i, sibling, dst, dst).wait_recv()

    def rows(q, x_, h_, c_, start, n):
        return sh.at[q, x_ * 4 + h_ * 2 + c_, pl.ds(start, n)]

    colour = lax.rem(z + 2 * l, 4)

    def quarter(q, x_, h_, k):
        return rows(q, x_, h_, c, pl.multiple_of(lax.rem(k, 4) * 48, 16), 48)

    def whole(q, x_, h_, c_):
        return sh.at[q, x_ * 4 + h_ * 2 + c_]

    def start_own(q):
        b = q * PER_PAIR
        send(b + XP0, to_xp, rows(q, x, h, c, 0, 96))
        send(b + XM0, to_xm, rows(q, x, h, c, 96, 96))
        send(b + XP1, to_xp, rows(q, x, h, c, 96, 96))
        send(b + XM1, to_xm, rows(q, x, h, c, 0, 96))
        send(b + OPP, opposite, quarter(q, x, h, colour + 2))
        send(b + SIB, sibling, whole(q, x, h, c))

    def second_hop(q):
        b = q * PER_PAIR
        recv(b + XP0, rows(q, xm, h, c, 0, 96))
        send(b + XP2, to_xp, rows(q, xm, h, c, 0, 96))
        recv(b + XM0, rows(q, xp, h, c, 96, 96))
        send(b + XM2, to_xm, rows(q, xp, h, c, 96, 96))

    def pass_on(q, j):
        b = q * PER_PAIR
        send(b + OPP + j, opposite, quarter(q, xs[j], h, colour + 2))
        send(b + SIB + j, sibling, whole(q, xs[j], h, c))

    def first_done(q):
        b = q * PER_PAIR
        recv(b + XP1, rows(q, xm, h, c, 96, 96))
        pass_on(q, 1)
        recv(b + XM1, rows(q, xp, h, c, 0, 96))
        pass_on(q, 2)

    def second_done(q):
        b = q * PER_PAIR
        recv(b + XP2, rows(q, xx, h, c, 0, 96))
        recv(b + XM2, rows(q, xx, h, c, 96, 96))
        pass_on(q, 3)

    def fan_out(q, j):
        b = q * PER_PAIR
        recv(b + OPP + j, quarter(q, xs[j], 1 - h, colour))
        for d in range(3):
            send(b + FAN + 4 * d + j, fans[d], quarter(q, xs[j], 1 - h, colour))

    def fanned(q, j):
        b = q * PER_PAIR
        for d, k in enumerate((2, 3, 1)):
            recv(b + FAN + 4 * d + j, quarter(q, xs[j], 1 - h, colour + k))
        send(b + SIB + 4 + j, sibling, whole(q, xs[j], 1 - h, c))

    def all_here(q):
        b = q * PER_PAIR
        for j in range(4):
            recv(b + SIB + j, whole(q, xs[j], h, 1 - c))
            recv(b + SIB + 4 + j, whole(q, xs[j], 1 - h, 1 - c))

    def pack(q, first, second):
        for g in range(3):
            for i, w in enumerate((first, second)):
                xpad[64 * i : 64 * i + 64, :C] = sum(
                    dot(spread[64 * k : 64 * k + 64, :], w[3 * g + k]) for k in range(3)
                )
            moved = pltpu.roll(xpad[64:128, :], 64, 1)
            at = slice(64 * g, 64 * g + 64)
            sh[q, s, at, :256] = xpad[0:64, :256].astype(BF)
            sh[q, s, at, 256:384] = (xpad[0:64, 256:] + moved[:, :128]).astype(BF)
            sh[q, s, at, 384:] = moved[:, 128:].astype(BF)

    def dot(a, b):
        return jnp.dot(a, b, preferred_element_type=F32)

    def join_up(q):
        place = {tap: i for i, tap in enumerate(rest_order(q))}
        for x_ in range(4):
            for g in range(3):
                parts = jnp.concatenate([sh[q, 4 * x_ + i, 64 * g : 64 * g + 64, :] for i in range(4)], axis=0)
                joined = dot(join[...], parts).astype(BF)
                for k in range(3):
                    tap, block = 3 * g + k, joined[80 * k : 80 * k + 80]
                    if x_ < 3:
                        wm[q, 256 * tap + 80 * x_ : 256 * tap + 80 * x_ + 80, :] = block
                    else:
                        wm[q, 256 * tap + 240 : 256 * tap + 256, :] = block[:16]
                        wr[q, 64 * place[tap] : 64 * place[tap] + 64, :] = block[16:]

    def prepare(a, n):
        row = lax.broadcasted_iota(jnp.int32, (n, CP), 0) & 15
        moved = (
            jnp.where(row == 0, 0.0, pltpu.roll(a, 1, 0)),
            a,
            jnp.where(row == 15, 0.0, pltpu.roll(a, n - 1, 0)),
        )
        for i in range(3):
            main[i, :n, :] = moved[i][:, :256].astype(BF)
        t0, t1, t2 = (m[:, 256:] for m in moved)
        rc[:n, :] = (t0 + pltpu.roll(t1, 64, 1)).astype(BF)
        later = jnp.concatenate([t2[16:], t2[:16]], axis=0)
        r2[:n, :] = (t2 + pltpu.roll(later, 64, 1)).astype(BF)

    def conv(q, second, m):
        lo = 256 if second else 0
        left = []
        for tap in range(9):
            a, b = tap_shift(q, tap)
            left.append(main[a, 16 * b : 16 * b + m, :])
        acc = dot(jnp.concatenate(left, axis=1), wm[q, :, lo : lo + CP])
        rest = [rc[16 * b : 16 * b + m, :] for b in range(3)] + [r2[:m, :], r2[32 : 32 + m, :64]]
        acc += dot(jnp.concatenate(rest, axis=1), wr[q, :, lo : lo + CP])
        if second:
            acc = pltpu.roll(acc, C, 1)
        return jnp.where(lax.broadcasted_iota(jnp.int32, (m, CP), 1) < C, acc, 0.0)

    def silu(v):
        return v / (1.0 + jnp.exp(-v))

    def view_first(v):
        xpad[16:272, :C] = views[TOK * v : TOK * v + TOK, :].astype(F32)
        xpad[16:272, C:] = jnp.zeros((TOK, CP - C), F32)
        prepare(xpad[:288, :], 288)
        xpad[16:272, :] = silu(conv(0, False, TOK))

    def view_second(v):
        prepare(xpad[:288, :], 288)
        acc = conv(0, True, TOK)
        vmid[v, :, :] = acc
        vmid[v, :, :C] = acc[:, :C] + views[TOK * v : TOK * v + TOK, :].astype(F32)

    def put_values(to, g, val):
        val = val.astype(BF)
        to[g, :, 0:128] = val[:, :128]
        to[g, :, 256:384] = val[:, 128:256]
        to[g, :, 512:576] = val[:, 256:320]

    def view_pairs(o):
        first, second = vf[o, :, :C], vf[o, :, 256:]
        kv[2 * o, :, :C] = dot(first, p2v_k[...]).astype(BF)
        put_values(vv, 2 * o, dot(first, p2v_v[...]))
        kv[2 * o + 1, :, :C] = dot(second, wks[...]).astype(BF)
        put_values(vv, 2 * o + 1, dot(second, wvs[...]))

    def pano_pairs(o):
        feat = pf[o, :, :C]
        kp[o, :, :C] = dot(feat, v2p_k[...]).astype(BF)
        put_values(vp, o, dot(feat, v2p_v[...]))

    def attend(keys, values, bias, sink):
        lane = lax.broadcasted_iota(jnp.int32, (TOK, 128), 1)
        for j in range(3):
            query, ks = qs[:, 128 * j : 128 * j + 128], keys(j)
            vs = jnp.concatenate(values(j), axis=0)
            halves = []
            for e in range(2 if j < 2 else 1):
                mine = (lane >= 64 * e) & (lane < 64 * e + 64)
                picked = jnp.where(mine, query, jnp.zeros_like(query))
                scores = [
                    lax.dot_general(picked, k, (((1,), (1,)), ((), ())), preferred_element_type=F32) for k in ks
                ]
                top = None
                for sc, b in zip(scores, bias, strict=True):
                    t = jnp.max(sc, axis=1, keepdims=True)
                    t = t if b is None else t + b
                    top = t if top is None else jnp.maximum(top, t)
                if sink:
                    top = jnp.maximum(top, 0.0)
                shares = [
                    jnp.exp(sc - (top if b is None else top - b)).astype(BF) for sc, b in zip(scores, bias, strict=True)
                ]
                both = dot(jnp.concatenate(shares, axis=1), vs)
                total = both[:, 128:]
                if sink:
                    total = total + jnp.exp(-top)
                halves.append(both[:, :128] / total)
            out = halves[0] if j == 2 else jnp.where(lane < 64, halves[0], halves[1])
            att[:, 128 * j : 128 * j + 128] = out.astype(BF)

    xpad[0:128, 256:] = jnp.zeros((128, 128), F32)
    pack(0, vc1, vc2)
    xext[32:288, 256:] = jnp.zeros((TOK, 128), BF)
    xext[32:288, :C] = dot(turn[...], pano[...]).astype(BF)
    pl.semaphore_wait(barrier, 8)
    start_own(0)
    send(HALO, sibling, xext.at[pl.ds(pl.multiple_of(32 + 224 * (1 - c), 16), 32)],
         xext.at[pl.ds(pl.multiple_of(288 * c, 16), 32)])
    send(HALO + 1, beyond, xext.at[pl.ds(pl.multiple_of(32 + 224 * c, 16), 32)],
         xext.at[pl.ds(pl.multiple_of(288 * (1 - c), 16), 32)])

    pack(1, pc1, pc2)
    xpad[0:16, :] = jnp.zeros((16, CP), F32)
    xpad[272:288, :] = jnp.zeros((16, CP), F32)
    for buf, n in ((kv, 6), (kp, 3)):
        for g in range(n):
            buf[g, :, 256:] = jnp.zeros((TOK, 128), BF)
    for buf, n in ((vv, 6), (vp, 3)):
        for g in range(n):
            for j in range(3):
                buf[g, :, 256 * j + 128 : 256 * j + 256] = jnp.ones((TOK, 128), BF)
            buf[g, :, 512:640] = jnp.zeros((TOK, 128), BF)
    qs[:, 256:] = jnp.zeros((TOK, 128), BF)
    for to, w in ((wks, p2v_k), (wvs, p2v_v)):
        to[0:64, :] = jnp.zeros((64, C), BF)
        to[64:384, :] = w[...]

    second_hop(0)
    start_own(1)
    fan_out(0, 0)
    first_done(0)
    second_done(0)
    fan_out(0, 1)
    fan_out(0, 2)
    fan_out(0, 3)
    second_hop(1)
    fan_out(1, 0)
    for j in range(4):
        fanned(0, j)
    first_done(1)
    fan_out(1, 1)
    fan_out(1, 2)
    all_here(0)

    join_up(0)
    second_done(1)
    view_first(0)
    fan_out(1, 3)
    for j in range(3):
        fanned(1, j)
    view_second(0)
    fanned(1, 3)
    view_first(1)
    view_second(1)
    f0, f1 = vmid[0], pltpu.roll(vmid[1], 64, 1)
    vf[1, :, :256] = f0[:, :256].astype(BF)
    vf[1, :, 256:384] = (f0[:, 256:] + f1[:, :128]).astype(BF)
    vf[1, :, 384:] = f1[:, 128:].astype(BF)
    send(VIEWS, sibling, vf.at[1], vf.at[2 * c])
    send(VIEWS + 1, beyond, vf.at[1], vf.at[2 * (1 - c)])
    view_pairs(1)

    recv(HALO, xext.at[pl.ds(pl.multiple_of(288 * (1 - c), 16), 32)])
    recv(HALO + 1, xext.at[pl.ds(pl.multiple_of(288 * c, 16), 32)])
    prepare(xext[...].astype(F32), 320)
    all_here(1)
    join_up(1)
    hidden = silu(conv(1, False, 288))
    prepare(hidden, 288)
    mid = conv(1, True, TOK) + xext[32:288, :].astype(F32)
    pmid[...] = mid
    pf[1] = mid.astype(BF)
    send(PANO, sibling, pf.at[1], pf.at[2 * c])
    send(PANO + 1, beyond, pf.at[1], pf.at[2 * (1 - c)])
    pano_pairs(1)

    recv(VIEWS, vf.at[2 * (1 - c)])
    recv(VIEWS + 1, vf.at[2 * c])
    view_pairs(0)
    view_pairs(2)
    qs[:, :C] = (dot(pf[1, :, :C], p2v_q[...]).astype(BF).astype(F32) * 0.125).astype(BF)
    bias = []
    for o in range(3):
        so = lax.rem(s + 15 + o, 16)
        for v in range(2):
            named = (links[2 * so + v, 0] == 2 - o) | (links[2 * so + v, 1] == 2 - o)
            bias.append(jnp.where(named & (count[so] > v), 0.0, NEG))
    attend(
        lambda j: [kv[g, :, 128 * j : 128 * j + 128] for g in range(6)],
        lambda j: [vv[g, :, 256 * j : 256 * j + 256] for g in range(6)],
        bias,
        True,
    )
    total = pmid[:, :C] + dot(att[:, :C], p2v_o[...])
    pano_out[...] = dot(turn[...], total.astype(BF)).astype(BF)

    recv(PANO, pf.at[2 * (1 - c)])
    recv(PANO + 1, pf.at[2 * c])
    pano_pairs(0)
    pano_pairs(2)
    for v in range(2):
        feat = vmid[v, :, :C].astype(BF)
        qs[:, :C] = (dot(feat, v2p_q[...]).astype(BF).astype(F32) * 0.125).astype(BF)
        a, b = links[2 * s + v, 0], links[2 * s + v, 1]
        attend(
            lambda j: [kp[i, :, 128 * j : 128 * j + 128] for i in (a, b)],
            lambda j: [vp[i, :, 256 * j : 256 * j + 256] for i in (a, b)],
            [None, None],
            False,
        )
        total = vmid[v, :, :C] + dot(att[:, :C], v2p_o[...])
        total = total * jnp.where(count[s] > v, 1.0, 0.0)
        view_out[TOK * v : TOK * v + TOK, :] = total.astype(BF)

    for cp in sent:
        cp.wait_send()


def spread_matrix():
    m = np.zeros((192, 20), np.float32)
    for k in range(3):
        for j in range(20):
            m[64 * k + 20 * k + j, j] = 1
    return m


def body(pano, views, count, links, pc1, pc2, vc1, vc2, *projections):
    vmem, smem = pl.BlockSpec(memory_space=pltpu.VMEM), pl.BlockSpec(memory_space=pltpu.SMEM)
    pano_out, view_out = pl.pallas_call(
        kernel,
        out_shape=(jax.ShapeDtypeStruct((TOK, C), BF), jax.ShapeDtypeStruct((2 * TOK, C), BF)),
        in_specs=[vmem] * 6 + [smem] * 2 + [vmem] * 11,
        out_specs=(vmem, vmem),
        scratch_shapes=[
            pltpu.VMEM((2, 16, SHARD, 2 * C), BF),
            pltpu.VMEM((2, 9 * 256, 2 * C), BF),
            pltpu.VMEM((2, 9 * 64, 2 * C), BF),
            pltpu.VMEM((3, 320, 256), BF),
            pltpu.VMEM((320, 128), BF),
            pltpu.VMEM((320, 128), BF),
            pltpu.VMEM((288, CP), F32),
            pltpu.VMEM((320, CP), BF),
            pltpu.VMEM((2, TOK, CP), F32),
            pltpu.VMEM((TOK, CP), F32),
            pltpu.VMEM((3, TOK, 2 * C), BF),
            pltpu.VMEM((3, TOK, CP), BF),
            pltpu.VMEM((CP, C), BF),
            pltpu.VMEM((CP, C), BF),
            pltpu.VMEM((6, TOK, CP), BF),
            pltpu.VMEM((6, TOK, 768), BF),
            pltpu.VMEM((3, TOK, CP), BF),
            pltpu.VMEM((3, TOK, 768), BF),
            pltpu.VMEM((TOK, CP), BF),
            pltpu.VMEM((TOK, CP), BF),
            pltpu.SemaphoreType.DMA((N_SEM,)),
            pltpu.SemaphoreType.DMA((N_SEM,)),
        ],
        compiler_params=pltpu.CompilerParams(
            collective_id=0, has_side_effects=True, vmem_limit_bytes=56 * 1024 * 1024
        ),
    )(
        pc1, pc2, vc1, vc2, pano.reshape(TOK, C), views.reshape(2 * TOK, C), count, links,
        jnp.asarray(turn_matrix(), BF), jnp.asarray(join_matrix(), BF), jnp.asarray(spread_matrix(), BF), *projections,
    )
    return pano_out.reshape(pano.shape), view_out.reshape(views.shape)


def solution(mesh):
    in_specs = (
        P("frame", "slab", None),
        P(("frame", "slab"), None, None, None),
        P("frame"),
        P("frame", None),
        *[P(None, "slab", None)] * 4,
        *[P()] * 8,
    )
    out_specs = (P("frame", "slab", None), P(("frame", "slab"), None, None, None))
    return jax.shard_map(body, mesh=mesh, in_specs=in_specs, out_specs=out_specs, check_vma=False)
```

```python
import jax
import jax.numpy as jnp
import numpy as np
from jax import lax
from jax.experimental import pallas as pl
from jax.experimental.pallas import tpu as pltpu
from jax.sharding import PartitionSpec as P

MESH = pl.DeviceIdType.MESH
F32, BF = jnp.float32, jnp.bfloat16
HEADS, C, CP, TOK = 5, 320, 384, 256
SHARD = 192
NEG = -1e30

XP0, XP1, XM0, XM1, XP2, XM2 = range(6)
OPP, FAN, SIB, PER_PAIR = 6, 10, 22, 30
HALO, VIEWS, PANO, N_SEM = 60, 62, 66, 68


def rest_order(pair):
    order = [(0, 0), (1, 0), (0, 1), (1, 1), (0, 2), (1, 2), (2, 0), (2, 1), (2, 2)]
    return [3 * b + a if pair == 0 else 3 * a + b for a, b in order]


def tap_shift(pair, tap):
    return (tap % 3, tap // 3) if pair == 0 else (tap // 3, tap % 3)


def turn_matrix():
    m = np.zeros((TOK, TOK), np.float32)
    for r in range(TOK):
        m[r, (r % 16) * 16 + r // 16] = 1
    return m


def join_matrix():
    m = np.zeros((240, 256), np.float32)
    for r in range(240):
        tap, u = r // 80, r % 80
        m[r, (u // 20) * 64 + tap * 20 + u % 20] = 1
    return m


def kernel(
    pc1, pc2, vc1, vc2, pano, views, count, links, turn, join, spread,
    p2v_q, p2v_k, p2v_v, p2v_o, v2p_q, v2p_k, v2p_v, v2p_o,
    pano_out, view_out,
    sh, wm, wr, main, rc, r2, xpad, xext, vmid, pmid, vf, pf, wks, wvs, kv, vv, kp, vp, qs, att, ss, rs,
):
    s, f = lax.axis_index("slab"), lax.axis_index("frame")
    x, h, c = lax.div(s, 4), lax.rem(lax.div(s, 2), 2), lax.rem(s, 2)
    l, z = lax.div(f, 16), lax.rem(f, 16)
    xm, xp, xx = lax.rem(x + 3, 4), lax.rem(x + 1, 4), lax.rem(x + 2, 4)
    xs = (x, xm, xp, xx)

    def dev(x_, h_, c_, l_, z_):
        return (l_ * 16 + z_, x_ * 4 + h_ * 2 + c_)

    to_xp, to_xm = dev(xp, h, c, l, z), dev(xm, h, c, l, z)
    opposite, same = dev(x, 1 - h, c, 1 - l, z), dev(x, h, c, 1 - l, z)
    to_zp, to_zm = dev(x, h, c, l, lax.rem(z + 1, 16)), dev(x, h, c, l, lax.rem(z + 15, 16))
    sibling = dev(x, h, 1 - c, l, z)
    beyond = (f, lax.rem(s + 15 + 2 * c, 16))
    fans = (same, to_zp, to_zm)

    barrier = pltpu.get_barrier_semaphore()
    for d in (to_xp, to_xm, opposite, same, to_zp, to_zm, sibling, beyond):
        pl.semaphore_signal(barrier, inc=1, device_id=d, device_id_type=MESH)

    sent = []

    def copy(i, to, src, dst):
        return pltpu.make_async_remote_copy(
            src_ref=src, dst_ref=dst, send_sem=ss.at[i], recv_sem=rs.at[i], device_id=to, device_id_type=MESH
        )

    def send(i, to, src, dst=None):
        cp = copy(i, to, src, src if dst is None else dst)
        cp.start()
        sent.append(cp)

    def recv(i, dst):
        copy(i, sibling, dst, dst).wait_recv()

    def rows(q, x_, h_, c_, start, n):
        return sh.at[q, x_ * 4 + h_ * 2 + c_, pl.ds(start, n)]

    colour = lax.rem(z + 2 * l, 4)

    def quarter(q, x_, h_, k):
        return rows(q, x_, h_, c, pl.multiple_of(lax.rem(k, 4) * 48, 16), 48)

    def whole(q, x_, h_, c_):
        return sh.at[q, x_ * 4 + h_ * 2 + c_]

    def start_own(q):
        b = q * PER_PAIR
        send(b + XP0, to_xp, rows(q, x, h, c, 0, 96))
        send(b + XM0, to_xm, rows(q, x, h, c, 96, 96))
        send(b + XP1, to_xp, rows(q, x, h, c, 96, 96))
        send(b + XM1, to_xm, rows(q, x, h, c, 0, 96))
        send(b + OPP, opposite, quarter(q, x, h, colour + 2))
        send(b + SIB, sibling, whole(q, x, h, c))

    def second_hop(q):
        b = q * PER_PAIR
        recv(b + XP0, rows(q, xm, h, c, 0, 96))
        send(b + XP2, to_xp, rows(q, xm, h, c, 0, 96))
        recv(b + XM0, rows(q, xp, h, c, 96, 96))
        send(b + XM2, to_xm, rows(q, xp, h, c, 96, 96))

    def pass_on(q, j):
        b = q * PER_PAIR
        send(b + OPP + j, opposite, quarter(q, xs[j], h, colour + 2))
        send(b + SIB + j, sibling, whole(q, xs[j], h, c))

    def first_done(q):
        b = q * PER_PAIR
        recv(b + XP1, rows(q, xm, h, c, 96, 96))
        pass_on(q, 1)
        recv(b + XM1, rows(q, xp, h, c, 0, 96))
        pass_on(q, 2)

    def second_done(q):
        b = q * PER_PAIR
        recv(b + XP2, rows(q, xx, h, c, 0, 96))
        recv(b + XM2, rows(q, xx, h, c, 96, 96))
        pass_on(q, 3)

    def fan_out(q, j):
        b = q * PER_PAIR
        recv(b + OPP + j, quarter(q, xs[j], 1 - h, colour))
        for d in range(3):
            send(b + FAN + 4 * d + j, fans[d], quarter(q, xs[j], 1 - h, colour))

    def fanned(q, j):
        b = q * PER_PAIR
        for d, k in enumerate((2, 3, 1)):
            recv(b + FAN + 4 * d + j, quarter(q, xs[j], 1 - h, colour + k))
        send(b + SIB + 4 + j, sibling, whole(q, xs[j], 1 - h, c))

    def all_here(q):
        b = q * PER_PAIR
        for j in range(4):
            recv(b + SIB + j, whole(q, xs[j], h, 1 - c))
            recv(b + SIB + 4 + j, whole(q, xs[j], 1 - h, 1 - c))

    def pack(q, first, second):
        for g in range(3):
            for i, w in enumerate((first, second)):
                xpad[64 * i : 64 * i + 64, :C] = sum(
                    dot(spread[64 * k : 64 * k + 64, :], w[3 * g + k]) for k in range(3)
                )
            moved = pltpu.roll(xpad[64:128, :], 64, 1)
            at = slice(64 * g, 64 * g + 64)
            sh[q, s, at, :256] = xpad[0:64, :256].astype(BF)
            sh[q, s, at, 256:384] = (xpad[0:64, 256:] + moved[:, :128]).astype(BF)
            sh[q, s, at, 384:] = moved[:, 128:].astype(BF)

    def dot(a, b):
        return jnp.dot(a, b, preferred_element_type=F32)

    def join_up(q):
        place = {tap: i for i, tap in enumerate(rest_order(q))}
        for x_ in range(4):
            for g in range(3):
                parts = jnp.concatenate([sh[q, 4 * x_ + i, 64 * g : 64 * g + 64, :] for i in range(4)], axis=0)
                joined = dot(join[...], parts).astype(BF)
                for k in range(3):
                    tap, block = 3 * g + k, joined[80 * k : 80 * k + 80]
                    if x_ < 3:
                        wm[q, 256 * tap + 80 * x_ : 256 * tap + 80 * x_ + 80, :] = block
                    else:
                        wm[q, 256 * tap + 240 : 256 * tap + 256, :] = block[:16]
                        wr[q, 64 * place[tap] : 64 * place[tap] + 64, :] = block[16:]

    def prepare(a, n):
        row = lax.broadcasted_iota(jnp.int32, (n, CP), 0) & 15
        moved = (
            jnp.where(row == 0, 0.0, pltpu.roll(a, 1, 0)),
            a,
            jnp.where(row == 15, 0.0, pltpu.roll(a, n - 1, 0)),
        )
        for i in range(3):
            main[i, :n, :] = moved[i][:, :256].astype(BF)
        t0, t1, t2 = (m[:, 256:] for m in moved)
        rc[:n, :] = (t0 + pltpu.roll(t1, 64, 1)).astype(BF)
        later = jnp.concatenate([t2[16:], t2[:16]], axis=0)
        r2[:n, :] = (t2 + pltpu.roll(later, 64, 1)).astype(BF)

    def conv(q, second, m):
        lo = 256 if second else 0
        left = []
        for tap in range(9):
            a, b = tap_shift(q, tap)
            left.append(main[a, 16 * b : 16 * b + m, :])
        acc = dot(jnp.concatenate(left, axis=1), wm[q, :, lo : lo + CP])
        rest = [rc[16 * b : 16 * b + m, :] for b in range(3)] + [r2[:m, :], r2[32 : 32 + m, :64]]
        acc += dot(jnp.concatenate(rest, axis=1), wr[q, :, lo : lo + CP])
        if second:
            acc = pltpu.roll(acc, C, 1)
        return jnp.where(lax.broadcasted_iota(jnp.int32, (m, CP), 1) < C, acc, 0.0)

    def silu(v):
        return v / (1.0 + jnp.exp(-v))

    def view_first(v):
        xpad[16:272, :C] = views[TOK * v : TOK * v + TOK, :].astype(F32)
        xpad[16:272, C:] = jnp.zeros((TOK, CP - C), F32)
        prepare(xpad[:288, :], 288)
        xpad[16:272, :] = silu(conv(0, False, TOK))

    def view_second(v):
        prepare(xpad[:288, :], 288)
        acc = conv(0, True, TOK)
        vmid[v, :, :] = acc
        vmid[v, :, :C] = acc[:, :C] + views[TOK * v : TOK * v + TOK, :].astype(F32)

    def put_values(to, g, val):
        val = val.astype(BF)
        to[g, :, 0:128] = val[:, :128]
        to[g, :, 256:384] = val[:, 128:256]
        to[g, :, 512:576] = val[:, 256:320]

    def view_pairs(o):
        first, second = vf[o, :, :C], vf[o, :, 256:]
        kv[2 * o, :, :C] = dot(first, p2v_k[...]).astype(BF)
        put_values(vv, 2 * o, dot(first, p2v_v[...]))
        kv[2 * o + 1, :, :C] = dot(second, wks[...]).astype(BF)
        put_values(vv, 2 * o + 1, dot(second, wvs[...]))

    def pano_pairs(o):
        feat = pf[o, :, :C]
        kp[o, :, :C] = dot(feat, v2p_k[...]).astype(BF)
        put_values(vp, o, dot(feat, v2p_v[...]))

    def attend(keys, values, bias, sink):
        lane = lax.broadcasted_iota(jnp.int32, (TOK, 128), 1)
        for j in range(3):
            query, ks = qs[:, 128 * j : 128 * j + 128], keys(j)
            vs = jnp.concatenate(values(j), axis=0)
            halves = []
            for e in range(2 if j < 2 else 1):
                mine = (lane >= 64 * e) & (lane < 64 * e + 64)
                picked = jnp.where(mine, query, jnp.zeros_like(query))
                scores = [
                    lax.dot_general(picked, k, (((1,), (1,)), ((), ())), preferred_element_type=F32) for k in ks
                ]
                top = None
                for sc, b in zip(scores, bias, strict=True):
                    t = jnp.max(sc, axis=1, keepdims=True)
                    t = t if b is None else t + b
                    top = t if top is None else jnp.maximum(top, t)
                if sink:
                    top = jnp.maximum(top, 0.0)
                shares = [
                    jnp.exp(sc - (top if b is None else top - b)).astype(BF) for sc, b in zip(scores, bias, strict=True)
                ]
                both = dot(jnp.concatenate(shares, axis=1), vs)
                total = both[:, 128:]
                if sink:
                    total = total + jnp.exp(-top)
                halves.append(both[:, :128] / total)
            out = halves[0] if j == 2 else jnp.where(lane < 64, halves[0], halves[1])
            att[:, 128 * j : 128 * j + 128] = out.astype(BF)

    def view_part(o, part):
        return vf.at[o, :, pl.ds(256, CP)] if part else vf.at[o, :, pl.ds(0, 256)]

    def send_views(part):
        send(VIEWS + 2 * part, sibling, view_part(1, part), view_part(2 * c, part))
        send(VIEWS + 2 * part + 1, beyond, view_part(1, part), view_part(2 * (1 - c), part))

    xpad[0:128, 256:] = jnp.zeros((128, 128), F32)
    pack(0, vc1, vc2)
    xext[32:288, 256:] = jnp.zeros((TOK, 128), BF)
    xext[32:288, :C] = dot(turn[...], pano[...]).astype(BF)
    pl.semaphore_wait(barrier, 8)
    start_own(0)
    send(HALO, sibling, xext.at[pl.ds(pl.multiple_of(32 + 224 * (1 - c), 16), 32)],
         xext.at[pl.ds(pl.multiple_of(288 * c, 16), 32)])
    send(HALO + 1, beyond, xext.at[pl.ds(pl.multiple_of(32 + 224 * c, 16), 32)],
         xext.at[pl.ds(pl.multiple_of(288 * (1 - c), 16), 32)])

    pack(1, pc1, pc2)
    xpad[0:16, :] = jnp.zeros((16, CP), F32)
    xpad[272:288, :] = jnp.zeros((16, CP), F32)
    for buf, n in ((kv, 6), (kp, 3)):
        for g in range(n):
            buf[g, :, 256:] = jnp.zeros((TOK, 128), BF)
    for buf, n in ((vv, 6), (vp, 3)):
        for g in range(n):
            for j in range(3):
                buf[g, :, 256 * j + 128 : 256 * j + 256] = jnp.ones((TOK, 128), BF)
            buf[g, :, 512:640] = jnp.zeros((TOK, 128), BF)
    qs[:, 256:] = jnp.zeros((TOK, 128), BF)
    for to, w in ((wks, p2v_k), (wvs, p2v_v)):
        to[0:64, :] = jnp.zeros((64, C), BF)
        to[64:384, :] = w[...]

    second_hop(0)
    start_own(1)
    fan_out(0, 0)
    first_done(0)
    second_done(0)
    fan_out(0, 1)
    fan_out(0, 2)
    fan_out(0, 3)
    second_hop(1)
    fan_out(1, 0)
    for j in range(4):
        fanned(0, j)
    first_done(1)
    fan_out(1, 1)
    fan_out(1, 2)
    all_here(0)

    join_up(0)
    second_done(1)
    view_first(0)
    fan_out(1, 3)
    for j in range(3):
        fanned(1, j)
    view_second(0)
    vf[1, :, :256] = vmid[0, :, :256].astype(BF)
    send_views(0)
    fanned(1, 3)
    view_first(1)
    view_second(1)
    f1 = pltpu.roll(vmid[1], 64, 1)
    vf[1, :, 256:384] = (vmid[0, :, 256:] + f1[:, :128]).astype(BF)
    vf[1, :, 384:] = f1[:, 128:].astype(BF)
    send_views(1)
    view_pairs(1)

    recv(HALO, xext.at[pl.ds(pl.multiple_of(288 * (1 - c), 16), 32)])
    recv(HALO + 1, xext.at[pl.ds(pl.multiple_of(288 * c, 16), 32)])
    prepare(xext[...].astype(F32), 320)
    all_here(1)
    join_up(1)
    hidden = silu(conv(1, False, 288))
    prepare(hidden, 288)
    mid = conv(1, True, TOK) + xext[32:288, :].astype(F32)
    pmid[...] = mid
    pf[1] = mid.astype(BF)
    send(PANO, sibling, pf.at[1], pf.at[2 * c])
    send(PANO + 1, beyond, pf.at[1], pf.at[2 * (1 - c)])
    pano_pairs(1)

    for part in range(2):
        recv(VIEWS + 2 * part, view_part(2 * (1 - c), part))
        recv(VIEWS + 2 * part + 1, view_part(2 * c, part))
    view_pairs(0)
    view_pairs(2)
    qs[:, :C] = (dot(pf[1, :, :C], p2v_q[...]).astype(BF).astype(F32) * 0.125).astype(BF)
    bias = []
    for o in range(3):
        so = lax.rem(s + 15 + o, 16)
        for v in range(2):
            named = (links[2 * so + v, 0] == 2 - o) | (links[2 * so + v, 1] == 2 - o)
            bias.append(jnp.where(named & (count[so] > v), 0.0, NEG))
    attend(
        lambda j: [kv[g, :, 128 * j : 128 * j + 128] for g in range(6)],
        lambda j: [vv[g, :, 256 * j : 256 * j + 256] for g in range(6)],
        bias,
        True,
    )
    total = pmid[:, :C] + dot(att[:, :C], p2v_o[...])
    pano_out[...] = dot(turn[...], total.astype(BF)).astype(BF)

    recv(PANO, pf.at[2 * (1 - c)])
    recv(PANO + 1, pf.at[2 * c])
    pano_pairs(0)
    pano_pairs(2)
    for v in range(2):
        feat = vmid[v, :, :C].astype(BF)
        qs[:, :C] = (dot(feat, v2p_q[...]).astype(BF).astype(F32) * 0.125).astype(BF)
        a, b = links[2 * s + v, 0], links[2 * s + v, 1]
        attend(
            lambda j: [kp[i, :, 128 * j : 128 * j + 128] for i in (a, b)],
            lambda j: [vp[i, :, 256 * j : 256 * j + 256] for i in (a, b)],
            [None, None],
            False,
        )
        total = vmid[v, :, :C] + dot(att[:, :C], v2p_o[...])
        total = total * jnp.where(count[s] > v, 1.0, 0.0)
        view_out[TOK * v : TOK * v + TOK, :] = total.astype(BF)

    for cp in sent:
        cp.wait_send()


def spread_matrix():
    m = np.zeros((192, 20), np.float32)
    for k in range(3):
        for j in range(20):
            m[64 * k + 20 * k + j, j] = 1
    return m


def body(pano, views, count, links, pc1, pc2, vc1, vc2, *projections):
    vmem, smem = pl.BlockSpec(memory_space=pltpu.VMEM), pl.BlockSpec(memory_space=pltpu.SMEM)
    pano_out, view_out = pl.pallas_call(
        kernel,
        out_shape=(jax.ShapeDtypeStruct((TOK, C), BF), jax.ShapeDtypeStruct((2 * TOK, C), BF)),
        in_specs=[vmem] * 6 + [smem] * 2 + [vmem] * 11,
        out_specs=(vmem, vmem),
        scratch_shapes=[
            pltpu.VMEM((2, 16, SHARD, 2 * C), BF),
            pltpu.VMEM((2, 9 * 256, 2 * C), BF),
            pltpu.VMEM((2, 9 * 64, 2 * C), BF),
            pltpu.VMEM((3, 320, 256), BF),
            pltpu.VMEM((320, 128), BF),
            pltpu.VMEM((320, 128), BF),
            pltpu.VMEM((288, CP), F32),
            pltpu.VMEM((320, CP), BF),
            pltpu.VMEM((2, TOK, CP), F32),
            pltpu.VMEM((TOK, CP), F32),
            pltpu.VMEM((3, TOK, 2 * C), BF),
            pltpu.VMEM((3, TOK, CP), BF),
            pltpu.VMEM((CP, C), BF),
            pltpu.VMEM((CP, C), BF),
            pltpu.VMEM((6, TOK, CP), BF),
            pltpu.VMEM((6, TOK, 768), BF),
            pltpu.VMEM((3, TOK, CP), BF),
            pltpu.VMEM((3, TOK, 768), BF),
            pltpu.VMEM((TOK, CP), BF),
            pltpu.VMEM((TOK, CP), BF),
            pltpu.SemaphoreType.DMA((N_SEM,)),
            pltpu.SemaphoreType.DMA((N_SEM,)),
        ],
        compiler_params=pltpu.CompilerParams(
            collective_id=0, has_side_effects=True, vmem_limit_bytes=56 * 1024 * 1024
        ),
    )(
        pc1, pc2, vc1, vc2, pano.reshape(TOK, C), views.reshape(2 * TOK, C), count, links,
        jnp.asarray(turn_matrix(), BF), jnp.asarray(join_matrix(), BF), jnp.asarray(spread_matrix(), BF), *projections,
    )
    return pano_out.reshape(pano.shape), view_out.reshape(views.shape)


def solution(mesh):
    in_specs = (
        P("frame", "slab", None),
        P(("frame", "slab"), None, None, None),
        P("frame"),
        P("frame", None),
        *[P(None, "slab", None)] * 4,
        *[P()] * 8,
    )
    out_specs = (P("frame", "slab", None), P(("frame", "slab"), None, None, None))
    return jax.shard_map(body, mesh=mesh, in_specs=in_specs, out_specs=out_specs, check_vma=False)
```

```python
import jax
import jax.numpy as jnp
import numpy as np
from jax import lax
from jax.experimental import pallas as pl
from jax.experimental.pallas import tpu as pltpu
from jax.sharding import PartitionSpec as P

MESH = pl.DeviceIdType.MESH
F32, BF = jnp.float32, jnp.bfloat16
HEADS, C, CP, TOK = 5, 320, 384, 256
SHARD = 192
NEG = -1e30

XP0, XP1, XM0, XM1, XP2, XM2 = range(6)
OPP, FAN, SIB, PER_PAIR = 6, 10, 22, 30
HALO, VIEWS, PANO, N_SEM = 60, 62, 66, 68


def rest_order(pair):
    order = [(0, 0), (1, 0), (0, 1), (1, 1), (0, 2), (1, 2), (2, 0), (2, 1), (2, 2)]
    return [3 * b + a if pair == 0 else 3 * a + b for a, b in order]


def tap_shift(pair, tap):
    return (tap % 3, tap // 3) if pair == 0 else (tap // 3, tap % 3)


def turn_matrix():
    m = np.zeros((TOK, TOK), np.float32)
    for r in range(TOK):
        m[r, (r % 16) * 16 + r // 16] = 1
    return m


def join_matrix():
    m = np.zeros((240, 256), np.float32)
    for r in range(240):
        tap, u = r // 80, r % 80
        m[r, (u // 20) * 64 + tap * 20 + u % 20] = 1
    return m


def kernel(
    pc1, pc2, vc1, vc2, pano, views, count, links, turn, join, spread,
    p2v_q, p2v_k, p2v_v, p2v_o, v2p_q, v2p_k, v2p_v, v2p_o,
    pano_out, view_out,
    sh, wm, wr, main, rc, r2, xpad, xext, vmid, pmid, vf, pf, wks, wvs, kv, vv, kp, vp, qs, att, ss, rs,
):
    s, f = lax.axis_index("slab"), lax.axis_index("frame")
    x, h, c = lax.div(s, 4), lax.rem(lax.div(s, 2), 2), lax.rem(s, 2)
    l, z = lax.div(f, 16), lax.rem(f, 16)
    xm, xp, xx = lax.rem(x + 3, 4), lax.rem(x + 1, 4), lax.rem(x + 2, 4)
    xs = (x, xm, xp, xx)

    def dev(x_, h_, c_, l_, z_):
        return (l_ * 16 + z_, x_ * 4 + h_ * 2 + c_)

    to_xp, to_xm = dev(xp, h, c, l, z), dev(xm, h, c, l, z)
    opposite, same = dev(x, 1 - h, c, 1 - l, z), dev(x, h, c, 1 - l, z)
    to_zp, to_zm = dev(x, h, c, l, lax.rem(z + 1, 16)), dev(x, h, c, l, lax.rem(z + 15, 16))
    sibling = dev(x, h, 1 - c, l, z)
    beyond = (f, lax.rem(s + 15 + 2 * c, 16))
    fans = (same, to_zp, to_zm)

    barrier = pltpu.get_barrier_semaphore()
    for d in (to_xp, to_xm, opposite, same, to_zp, to_zm, sibling, beyond):
        pl.semaphore_signal(barrier, inc=1, device_id=d, device_id_type=MESH)

    sent = []

    def copy(i, to, src, dst):
        return pltpu.make_async_remote_copy(
            src_ref=src, dst_ref=dst, send_sem=ss.at[i], recv_sem=rs.at[i], device_id=to, device_id_type=MESH
        )

    def send(i, to, src, dst=None):
        cp = copy(i, to, src, src if dst is None else dst)
        cp.start()
        sent.append(cp)

    def recv(i, dst):
        copy(i, sibling, dst, dst).wait_recv()

    def rows(q, x_, h_, c_, start, n):
        return sh.at[q, x_ * 4 + h_ * 2 + c_, pl.ds(start, n)]

    colour = lax.rem(z + 2 * l, 4)

    def quarter(q, x_, h_, k):
        return rows(q, x_, h_, c, pl.multiple_of(lax.rem(k, 4) * 48, 16), 48)

    def whole(q, x_, h_, c_):
        return sh.at[q, x_ * 4 + h_ * 2 + c_]

    def start_own(q):
        b = q * PER_PAIR
        send(b + XP0, to_xp, rows(q, x, h, c, 0, 96))
        send(b + XM0, to_xm, rows(q, x, h, c, 96, 96))
        send(b + XP1, to_xp, rows(q, x, h, c, 96, 96))
        send(b + XM1, to_xm, rows(q, x, h, c, 0, 96))
        send(b + OPP, opposite, quarter(q, x, h, colour + 2))
        send(b + SIB, sibling, whole(q, x, h, c))

    def second_hop(q):
        b = q * PER_PAIR
        recv(b + XP0, rows(q, xm, h, c, 0, 96))
        send(b + XP2, to_xp, rows(q, xm, h, c, 0, 96))
        recv(b + XM0, rows(q, xp, h, c, 96, 96))
        send(b + XM2, to_xm, rows(q, xp, h, c, 96, 96))

    def pass_on(q, j):
        b = q * PER_PAIR
        send(b + OPP + j, opposite, quarter(q, xs[j], h, colour + 2))
        send(b + SIB + j, sibling, whole(q, xs[j], h, c))

    def first_done(q):
        b = q * PER_PAIR
        recv(b + XP1, rows(q, xm, h, c, 96, 96))
        pass_on(q, 1)
        recv(b + XM1, rows(q, xp, h, c, 0, 96))
        pass_on(q, 2)

    def second_done(q):
        b = q * PER_PAIR
        recv(b + XP2, rows(q, xx, h, c, 0, 96))
        recv(b + XM2, rows(q, xx, h, c, 96, 96))
        pass_on(q, 3)

    def fan_out(q, j):
        b = q * PER_PAIR
        recv(b + OPP + j, quarter(q, xs[j], 1 - h, colour))
        for d in range(3):
            send(b + FAN + 4 * d + j, fans[d], quarter(q, xs[j], 1 - h, colour))

    def fanned(q, j):
        b = q * PER_PAIR
        for d, k in enumerate((2, 3, 1)):
            recv(b + FAN + 4 * d + j, quarter(q, xs[j], 1 - h, colour + k))
        send(b + SIB + 4 + j, sibling, whole(q, xs[j], 1 - h, c))

    def all_here(q):
        b = q * PER_PAIR
        for j in range(4):
            recv(b + SIB + j, whole(q, xs[j], h, 1 - c))
            recv(b + SIB + 4 + j, whole(q, xs[j], 1 - h, 1 - c))

    def pack(q, first, second):
        for g in range(3):
            for i, w in enumerate((first, second)):
                xpad[64 * i : 64 * i + 64, :C] = sum(
                    dot(spread[64 * k : 64 * k + 64, :], w[3 * g + k]) for k in range(3)
                )
            moved = pltpu.roll(xpad[64:128, :], 64, 1)
            at = slice(64 * g, 64 * g + 64)
            sh[q, s, at, :256] = xpad[0:64, :256].astype(BF)
            sh[q, s, at, 256:384] = (xpad[0:64, 256:] + moved[:, :128]).astype(BF)
            sh[q, s, at, 384:] = moved[:, 128:].astype(BF)

    def dot(a, b):
        return jnp.dot(a, b, preferred_element_type=F32)

    def join_up(q):
        place = {tap: i for i, tap in enumerate(rest_order(q))}
        for x_ in range(4):
            for g in range(3):
                parts = jnp.concatenate([sh[q, 4 * x_ + i, 64 * g : 64 * g + 64, :] for i in range(4)], axis=0)
                joined = dot(join[...], parts).astype(BF)
                for k in range(3):
                    tap, block = 3 * g + k, joined[80 * k : 80 * k + 80]
                    if x_ < 3:
                        wm[q, 256 * tap + 80 * x_ : 256 * tap + 80 * x_ + 80, :] = block
                    else:
                        wm[q, 256 * tap + 240 : 256 * tap + 256, :] = block[:16]
                        wr[q, 64 * place[tap] : 64 * place[tap] + 64, :] = block[16:]

    def prepare(a, n):
        row = lax.broadcasted_iota(jnp.int32, (n, CP), 0) & 15
        moved = (
            jnp.where(row == 0, 0.0, pltpu.roll(a, 1, 0)),
            a,
            jnp.where(row == 15, 0.0, pltpu.roll(a, n - 1, 0)),
        )
        for i in range(3):
            main[i, :n, :] = moved[i][:, :256].astype(BF)
        t0, t1, t2 = (m[:, 256:] for m in moved)
        rc[:n, :] = (t0 + pltpu.roll(t1, 64, 1)).astype(BF)
        later = jnp.concatenate([t2[16:], t2[:16]], axis=0)
        r2[:n, :] = (t2 + pltpu.roll(later, 64, 1)).astype(BF)

    def conv(q, second, m):
        lo = 256 if second else 0
        left = []
        for tap in range(9):
            a, b = tap_shift(q, tap)
            left.append(main[a, 16 * b : 16 * b + m, :])
        acc = dot(jnp.concatenate(left, axis=1), wm[q, :, lo : lo + CP])
        rest = [rc[16 * b : 16 * b + m, :] for b in range(3)] + [r2[:m, :], r2[32 : 32 + m, :64]]
        acc += dot(jnp.concatenate(rest, axis=1), wr[q, :, lo : lo + CP])
        if second:
            acc = pltpu.roll(acc, C, 1)
        return jnp.where(lax.broadcasted_iota(jnp.int32, (m, CP), 1) < C, acc, 0.0)

    def silu(v):
        return v / (1.0 + jnp.exp(-v))

    def view_first(v):
        xpad[16:272, :C] = views[TOK * v : TOK * v + TOK, :].astype(F32)
        xpad[16:272, C:] = jnp.zeros((TOK, CP - C), F32)
        prepare(xpad[:288, :], 288)
        xpad[16:272, :] = silu(conv(0, False, TOK))

    def view_second(v):
        prepare(xpad[:288, :], 288)
        acc = conv(0, True, TOK)
        vmid[v, :, :] = acc
        vmid[v, :, :C] = acc[:, :C] + views[TOK * v : TOK * v + TOK, :].astype(F32)

    def put_values(to, g, val):
        val = val.astype(BF)
        to[g, :, 0:128] = val[:, :128]
        to[g, :, 256:384] = val[:, 128:256]
        to[g, :, 512:576] = val[:, 256:320]

    def view_pairs(o):
        first, second = vf[o, :, :C], vf[o, :, 256:]
        kv[2 * o, :, :C] = dot(first, p2v_k[...]).astype(BF)
        put_values(vv, 2 * o, dot(first, p2v_v[...]))
        kv[2 * o + 1, :, :C] = dot(second, wks[...]).astype(BF)
        put_values(vv, 2 * o + 1, dot(second, wvs[...]))

    def pano_pairs(o):
        feat = pf[o, :, :C]
        kp[o, :, :C] = dot(feat, v2p_k[...]).astype(BF)
        put_values(vp, o, dot(feat, v2p_v[...]))

    def attend(keys, values, bias, sink):
        lane = lax.broadcasted_iota(jnp.int32, (TOK, 128), 1)
        for j in range(3):
            query, ks = qs[:, 128 * j : 128 * j + 128], keys(j)
            vs = jnp.concatenate(values(j), axis=0)
            halves = []
            for e in range(2 if j < 2 else 1):
                mine = (lane >= 64 * e) & (lane < 64 * e + 64)
                picked = jnp.where(mine, query, jnp.zeros_like(query))
                scores = [
                    lax.dot_general(picked, k, (((1,), (1,)), ((), ())), preferred_element_type=F32) for k in ks
                ]
                top = None
                for sc, b in zip(scores, bias, strict=True):
                    t = jnp.max(sc, axis=1, keepdims=True)
                    t = t if b is None else t + b
                    top = t if top is None else jnp.maximum(top, t)
                if sink:
                    top = jnp.maximum(top, 0.0)
                shares = [
                    jnp.exp(sc - (top if b is None else top - b)).astype(BF) for sc, b in zip(scores, bias, strict=True)
                ]
                both = dot(jnp.concatenate(shares, axis=1), vs)
                total = both[:, 128:]
                if sink:
                    total = total + jnp.exp(-top)
                halves.append(both[:, :128] / total)
            out = halves[0] if j == 2 else jnp.where(lane < 64, halves[0], halves[1])
            att[:, 128 * j : 128 * j + 128] = out.astype(BF)

    def view_part(o, part):
        return vf.at[o, :, pl.ds(256, CP)] if part else vf.at[o, :, pl.ds(0, 256)]

    def send_views(part):
        send(VIEWS + 2 * part, sibling, view_part(1, part), view_part(2 * c, part))
        send(VIEWS + 2 * part + 1, beyond, view_part(1, part), view_part(2 * (1 - c), part))

    xpad[0:128, 256:] = jnp.zeros((128, 128), F32)
    pack(0, vc1, vc2)
    xext[32:288, 256:] = jnp.zeros((TOK, 128), BF)
    xext[32:288, :C] = dot(turn[...], pano[...]).astype(BF)
    pl.semaphore_wait(barrier, 8)
    start_own(0)
    send(HALO, sibling, xext.at[pl.ds(pl.multiple_of(32 + 224 * (1 - c), 16), 32)],
         xext.at[pl.ds(pl.multiple_of(288 * c, 16), 32)])
    send(HALO + 1, beyond, xext.at[pl.ds(pl.multiple_of(32 + 224 * c, 16), 32)],
         xext.at[pl.ds(pl.multiple_of(288 * (1 - c), 16), 32)])

    pack(1, pc1, pc2)
    xpad[0:16, :] = jnp.zeros((16, CP), F32)
    xpad[272:288, :] = jnp.zeros((16, CP), F32)
    for buf, n in ((kv, 6), (kp, 3)):
        for g in range(n):
            buf[g, :, 256:] = jnp.zeros((TOK, 128), BF)
    for buf, n in ((vv, 6), (vp, 3)):
        for g in range(n):
            for j in range(3):
                buf[g, :, 256 * j + 128 : 256 * j + 256] = jnp.ones((TOK, 128), BF)
            buf[g, :, 512:640] = jnp.zeros((TOK, 128), BF)
    qs[:, 256:] = jnp.zeros((TOK, 128), BF)
    for to, w in ((wks, p2v_k), (wvs, p2v_v)):
        to[0:64, :] = jnp.zeros((64, C), BF)
        to[64:384, :] = w[...]

    second_hop(0)
    fan_out(0, 0)
    first_done(0)
    start_own(1)
    second_done(0)
    fan_out(0, 1)
    fan_out(0, 2)
    fan_out(0, 3)
    second_hop(1)
    fan_out(1, 0)
    for j in range(4):
        fanned(0, j)
    first_done(1)
    fan_out(1, 1)
    fan_out(1, 2)
    all_here(0)

    join_up(0)
    second_done(1)
    view_first(0)
    fan_out(1, 3)
    for j in range(3):
        fanned(1, j)
    view_second(0)
    vf[1, :, :256] = vmid[0, :, :256].astype(BF)
    send_views(0)
    fanned(1, 3)
    view_first(1)
    view_second(1)
    f1 = pltpu.roll(vmid[1], 64, 1)
    vf[1, :, 256:384] = (vmid[0, :, 256:] + f1[:, :128]).astype(BF)
    vf[1, :, 384:] = f1[:, 128:].astype(BF)
    send_views(1)
    view_pairs(1)

    recv(HALO, xext.at[pl.ds(pl.multiple_of(288 * (1 - c), 16), 32)])
    recv(HALO + 1, xext.at[pl.ds(pl.multiple_of(288 * c, 16), 32)])
    prepare(xext[...].astype(F32), 320)
    all_here(1)
    join_up(1)
    hidden = silu(conv(1, False, 288))
    prepare(hidden, 288)
    mid = conv(1, True, TOK) + xext[32:288, :].astype(F32)
    pmid[...] = mid
    pf[1] = mid.astype(BF)
    send(PANO, sibling, pf.at[1], pf.at[2 * c])
    send(PANO + 1, beyond, pf.at[1], pf.at[2 * (1 - c)])
    pano_pairs(1)

    for part in range(2):
        recv(VIEWS + 2 * part, view_part(2 * (1 - c), part))
        recv(VIEWS + 2 * part + 1, view_part(2 * c, part))
    view_pairs(0)
    view_pairs(2)
    qs[:, :C] = (dot(pf[1, :, :C], p2v_q[...]).astype(BF).astype(F32) * 0.125).astype(BF)
    bias = []
    for o in range(3):
        so = lax.rem(s + 15 + o, 16)
        for v in range(2):
            named = (links[2 * so + v, 0] == 2 - o) | (links[2 * so + v, 1] == 2 - o)
            bias.append(jnp.where(named & (count[so] > v), 0.0, NEG))
    attend(
        lambda j: [kv[g, :, 128 * j : 128 * j + 128] for g in range(6)],
        lambda j: [vv[g, :, 256 * j : 256 * j + 256] for g in range(6)],
        bias,
        True,
    )
    total = pmid[:, :C] + dot(att[:, :C], p2v_o[...])
    pano_out[...] = dot(turn[...], total.astype(BF)).astype(BF)

    recv(PANO, pf.at[2 * (1 - c)])
    recv(PANO + 1, pf.at[2 * c])
    pano_pairs(0)
    pano_pairs(2)
    for v in range(2):
        feat = vmid[v, :, :C].astype(BF)
        qs[:, :C] = (dot(feat, v2p_q[...]).astype(BF).astype(F32) * 0.125).astype(BF)
        a, b = links[2 * s + v, 0], links[2 * s + v, 1]
        attend(
            lambda j: [kp[i, :, 128 * j : 128 * j + 128] for i in (a, b)],
            lambda j: [vp[i, :, 256 * j : 256 * j + 256] for i in (a, b)],
            [None, None],
            False,
        )
        total = vmid[v, :, :C] + dot(att[:, :C], v2p_o[...])
        total = total * jnp.where(count[s] > v, 1.0, 0.0)
        view_out[TOK * v : TOK * v + TOK, :] = total.astype(BF)

    for cp in sent:
        cp.wait_send()


def spread_matrix():
    m = np.zeros((192, 20), np.float32)
    for k in range(3):
        for j in range(20):
            m[64 * k + 20 * k + j, j] = 1
    return m


def body(pano, views, count, links, pc1, pc2, vc1, vc2, *projections):
    vmem, smem = pl.BlockSpec(memory_space=pltpu.VMEM), pl.BlockSpec(memory_space=pltpu.SMEM)
    pano_out, view_out = pl.pallas_call(
        kernel,
        out_shape=(jax.ShapeDtypeStruct((TOK, C), BF), jax.ShapeDtypeStruct((2 * TOK, C), BF)),
        in_specs=[vmem] * 6 + [smem] * 2 + [vmem] * 11,
        out_specs=(vmem, vmem),
        scratch_shapes=[
            pltpu.VMEM((2, 16, SHARD, 2 * C), BF),
            pltpu.VMEM((2, 9 * 256, 2 * C), BF),
            pltpu.VMEM((2, 9 * 64, 2 * C), BF),
            pltpu.VMEM((3, 320, 256), BF),
            pltpu.VMEM((320, 128), BF),
            pltpu.VMEM((320, 128), BF),
            pltpu.VMEM((288, CP), F32),
            pltpu.VMEM((320, CP), BF),
            pltpu.VMEM((2, TOK, CP), F32),
            pltpu.VMEM((TOK, CP), F32),
            pltpu.VMEM((3, TOK, 2 * C), BF),
            pltpu.VMEM((3, TOK, CP), BF),
            pltpu.VMEM((CP, C), BF),
            pltpu.VMEM((CP, C), BF),
            pltpu.VMEM((6, TOK, CP), BF),
            pltpu.VMEM((6, TOK, 768), BF),
            pltpu.VMEM((3, TOK, CP), BF),
            pltpu.VMEM((3, TOK, 768), BF),
            pltpu.VMEM((TOK, CP), BF),
            pltpu.VMEM((TOK, CP), BF),
            pltpu.SemaphoreType.DMA((N_SEM,)),
            pltpu.SemaphoreType.DMA((N_SEM,)),
        ],
        compiler_params=pltpu.CompilerParams(
            collective_id=0, has_side_effects=True, vmem_limit_bytes=56 * 1024 * 1024
        ),
    )(
        pc1, pc2, vc1, vc2, pano.reshape(TOK, C), views.reshape(2 * TOK, C), count, links,
        jnp.asarray(turn_matrix(), BF), jnp.asarray(join_matrix(), BF), jnp.asarray(spread_matrix(), BF), *projections,
    )
    return pano_out.reshape(pano.shape), view_out.reshape(views.shape)


def solution(mesh):
    in_specs = (
        P("frame", "slab", None),
        P(("frame", "slab"), None, None, None),
        P("frame"),
        P("frame", None),
        *[P(None, "slab", None)] * 4,
        *[P()] * 8,
    )
    out_specs = (P("frame", "slab", None), P(("frame", "slab"), None, None, None))
    return jax.shard_map(body, mesh=mesh, in_specs=in_specs, out_specs=out_specs, check_vma=False)
```
